768 devices in a mesh: mp: 48 (over y, z_hi, core), tokens: 16 (over z_lo, x).
Axes of the slice: x: 4, y: 8, z: 12 (z_hi: 3, z_lo: 4; z = z_hi * 4 + z_lo), core: 2. Of those that a mesh axis runs over, the one named last changes fastest.
Arguments:
- tokens_in: bfloat16 [3072, 5120], P(('tokens', 'mp')), may hold values from -6 to 6
- grad_out: bfloat16 [3072, 5120], P(('tokens', 'mp')), may hold values from -6 to 6
- pre_act: bfloat16 [3072, 13824], P('tokens', 'mp'), may hold values from -6 to 6
- w_in: bfloat16 [5120, 13824], P(None, 'mp'), may hold values from -0.078125 to 0.078125
- w_out: bfloat16 [13824, 5120], P('mp'), may hold values from -0.0546875 to 0.0546875
Outputs:
- grad_in: bfloat16 [3072, 5120], P(('tokens', 'mp'))
- grad_w_in: bfloat16 [5120, 13824], P('tokens', 'mp')
- grad_w_out: bfloat16 [13824, 5120], P('mp', 'tokens')
The draws below stay inside these ranges and needn't reach their ends.
All inputs are finite; a program needn't handle non-finite values.
Results may differ from the reference program's by a relative error of at most 0.023.
Values may be sent and summed in bfloat16 or wider, within the bound.
A program may use at most 64 MiB of HBM per device.

```python
import math
import jax
import jax.numpy as jnp
from jax import lax

D = 5120
FF = 13824
TOKENS = 3072
N_TOKENS = 16


def block_levels(rng, shape, pieces, low, largest):
    factor_of = 1.0
    for position, parts in pieces:
        draws = jax.random.uniform(jax.random.fold_in(jax.random.fold_in(rng, 6), position), (parts,), jnp.float32, low / len(pieces), largest / len(pieces))
        factor_of = factor_of * jnp.repeat(jnp.exp(draws), shape[position] // parts).reshape((-1,) + (1,) * (len(shape) - 1 - position))
    return factor_of


def gaussian(own_key, shape, scale, most, shards=(), kind=jnp.bfloat16):
    gain = block_levels(own_key, shape, shards, -0.22, 0.18) if shards else 1.0
    values = jax.random.normal(own_key, shape, jnp.float32) * scale * gain
    return jnp.minimum(jnp.maximum(values, -most), most).astype(kind)


def setup_inputs(seed: int = 0) -> dict:
    arg_keys = jax.random.split(jax.random.key(seed), 6)
    return {
        "tokens_in": gaussian(arg_keys[0], (TOKENS, D), 1.0, 6.0, ((0, 768),)),
        "grad_out": gaussian(arg_keys[1], (TOKENS, D), 1.0, 6.0, ((0, 768),)),
        "pre_act": gaussian(arg_keys[2], (TOKENS, FF), 1.0, 6.0, ((0, 16), (1, 48))),
        "w_in": gaussian(arg_keys[3], (D, FF), D ** -0.5, 0.078125, ((1, 48),)),
        "w_out": gaussian(arg_keys[4], (FF, D), FF ** -0.5, 0.0546875, ((0, 48),)),
    }


root_two_pi = math.sqrt(2.0 / math.pi)
cubic = 0.044715

def gelu_value(pre):
    inner = root_two_pi * (pre + cubic * pre * pre * pre)
    return 0.5 * pre * (1.0 + jnp.tanh(inner))

def gelu_slope(pre):
    tanh_val = jnp.tanh(root_two_pi * (pre + cubic * pre * pre * pre))
    return 0.5 * (1.0 + tanh_val) + 0.5 * pre * (1.0 - tanh_val * tanh_val) * root_two_pi * (1.0 + 3.0 * cubic * pre * pre)

def reference(tokens_in, grad_out, pre_act, w_in, w_out):
    pre = pre_act.astype(jnp.float32)
    activated = gelu_value(pre).astype(jnp.bfloat16)
    slope = gelu_slope(pre)
    grad_act = jnp.dot(grad_out, w_out.T, preferred_element_type=jnp.float32)
    grad_pre = (grad_act * slope).astype(jnp.bfloat16)
    grad_in = jnp.dot(grad_pre, w_in.T, preferred_element_type=jnp.float32).astype(jnp.bfloat16)
    scale_back = 1.0 / math.sqrt(TOKENS)
    groups = N_TOKENS
    rows_per = TOKENS // groups
    x_groups = tokens_in.reshape(groups, rows_per, tokens_in.shape[1])
    g_groups = grad_out.reshape(groups, rows_per, grad_out.shape[1])
    p_groups = grad_pre.reshape(groups, rows_per, grad_pre.shape[1])
    a_groups = activated.reshape(groups, rows_per, activated.shape[1])

    def add_group(carry, items):
        x_rows, g_rows, p_rows, a_rows = items
        part_in = (jnp.dot(x_rows.T, p_rows, preferred_element_type=jnp.float32) * scale_back).astype(jnp.bfloat16)
        part_out = (jnp.dot(a_rows.T, g_rows, preferred_element_type=jnp.float32) * scale_back).astype(jnp.bfloat16)
        return ((carry[0] + part_in.astype(jnp.float32), carry[1] + part_out.astype(jnp.float32)), None)
    start = (jnp.zeros(w_in.shape, jnp.float32), jnp.zeros(w_out.shape, jnp.float32))
    sums, unused = lax.scan(add_group, start, (x_groups, g_groups, p_groups, a_groups))
    return (grad_in, sums[0].astype(jnp.bfloat16), sums[1].astype(jnp.bfloat16))
```

```python
import math

import jax
import jax.numpy as jnp
from jax import lax
from jax.experimental import pallas as pl
from jax.experimental.pallas import tpu as pltpu
from jax.sharding import PartitionSpec as P

root_two_pi = math.sqrt(2.0 / math.pi)
cubic = 0.044715

NY, NZ, NC = 8, 3, 2
NL, NX = 4, 4
ROWS = 4
BLK = ROWS * NX
NB = NY * NZ
NBLK = NC * NB
QB = NBLK // NX
QR = QB * BLK
WIDE = 5120
HID = 288
DQ = WIDE // NX
DP = DQ // NL
WIN = 384
MESH = pl.DeviceIdType.MESH
f32 = jnp.float32
bf16 = jnp.bfloat16


def gelu_value(pre):
    inner = root_two_pi * (pre + cubic * pre * pre * pre)
    return 0.5 * pre * (1.0 + jnp.tanh(inner))


def gelu_slope(pre):
    tanh_val = jnp.tanh(root_two_pi * (pre + cubic * pre * pre * pre))
    return 0.5 * (1.0 + tanh_val) + 0.5 * pre * (1.0 - tanh_val * tanh_val) * root_two_pi * (
        1.0 + 3.0 * cubic * pre * pre
    )


def kernel(
    go_ref, ti_ref, pre_ref, wo_ref, wi_ref,
    gin_ref, gwi_ref, gwo_ref,
    xsrc, xbuf, mbuf, gbuf, wwin, wsel, prebuf, pref, act, pbuf, gaown, rsbuf, gpbuf,
    wchunk, wrecv, gown, gsend, grecv, rsend, rrecv, zown, zsend, zrecv, fbuf, osrc, obuf,
    send_sem, x_sem, pre_sem, zg_sem, y_sem, sib_sem, w_sem, rs_sem, ag_sem, wr_sem,
    gs_sem, ry_sem, rz_sem, ro_sem,
):
    m = lax.axis_index("mp")
    t = lax.axis_index("tokens")
    c = lax.rem(m, NC)
    zh = lax.rem(m // NC, NZ)
    y = m // (NC * NZ)
    x = lax.rem(t, NX)
    zl = t // NX
    sg = 1 - 2 * c

    def at(y_=None, zh_=None, c_=None, zl_=None, x_=None):
        y_ = y if y_ is None else y_
        zh_ = zh if zh_ is None else zh_
        c_ = c if c_ is None else c_
        zl_ = zl if zl_ is None else zl_
        x_ = x if x_ is None else x_
        return {"mp": (y_ * NZ + zh_) * NC + c_, "tokens": zl_ * NX + x_}

    def ring(v, n):
        return lax.rem(v + n, n)

    other = 1 - c
    xs = [lax.rem(x + d, NX) for d in range(1, NX)]
    zhs = [lax.rem(zh + d, NZ) for d in range(1, NZ)]
    zls = [lax.rem(zl + d, NL) for d in range(1, NL)]
    fwd = at(y_=ring(y + sg, NY))
    bwd = at(y_=ring(y - sg, NY))
    sib = at(c_=other)
    flying = []

    def send(src, dst, sem, dev):
        cp = pltpu.make_async_remote_copy(
            src_ref=src, dst_ref=dst, send_sem=send_sem.at[len(flying)], recv_sem=sem,
            device_id=dev, device_id_type=MESH,
        )
        cp.start()
        flying.append(cp)

    def arrive(dst, sem):
        pltpu.make_async_remote_copy(
            src_ref=dst, dst_ref=dst, send_sem=send_sem.at[0], recv_sem=sem,
            device_id=sib, device_id_type=MESH,
        ).wait_recv()

    base = x * DP
    low = pl.multiple_of((base // 128) * 128, 128)
    odd = lax.rem(x, 2)
    loads = []
    for i, w in enumerate((wo_ref, wi_ref)):
        for k in range(NL):
            cp = pltpu.make_async_copy(
                w.at[:, pl.ds(pl.multiple_of(low + k * DQ, 128), WIN)], wwin.at[i, k], w_sem.at[i, k]
            )
            cp.start()
            loads.append(cp)

    for a, ref in enumerate((go_ref, ti_ref)):
        v = ref[...].astype(f32)
        for p in range(NX):
            xsrc[a, p] = jnp.concatenate(
                [v[:, k * DQ + p * DP : k * DQ + (p + 1) * DP] for k in range(NL)], axis=1
            ).astype(bf16)

    barrier = pltpu.get_barrier_semaphore()
    peers = (
        [at(x_=v) for v in xs] + [at(zh_=v) for v in zhs] + [at(zl_=v) for v in zls]
        + [fwd, bwd, sib]
    )
    for dev in peers:
        pl.semaphore_signal(barrier, inc=1, device_id=dev, device_id_type=MESH)
    pl.semaphore_wait(barrier, len(peers))

    for a in range(2):
        for v in xs:
            send(xsrc.at[a, v], xbuf.at[a, x], x_sem.at[a, x], at(x_=v))
    for v in xs:
        send(pre_ref, prebuf.at[x], pre_sem.at[x], at(x_=v))

    def block(y_, zh_, c_):
        return c_ * NB + y_ * NZ + zh_

    def merge(a):
        for v in xs:
            arrive(xbuf.at[a, v], x_sem.at[a, v])
        xbuf[a, pl.ds(x, 1)] = xsrc[a, pl.ds(x, 1)]
        for p in range(NX):
            mbuf[ROWS * p : ROWS * (p + 1)] = xbuf[a, p].astype(f32)
        gbuf[a, pl.ds(block(y, zh, c), 1)] = mbuf[...].astype(bf16)[None]
        mine = gbuf.at[a, block(y, zh, c)]
        for i, v in enumerate(zhs):
            send(mine, mine, zg_sem.at[a, zh], at(zh_=v))

    def hop(a, d, s, y_, zh_):
        ref = gbuf.at[a, block(y_, zh_, c)]
        send(ref, ref, y_sem.at[a, d, s, zh_], fwd if d == 0 else bwd)

    def to_sib(a, y_):
        ref = gbuf.at[a, pl.ds(block(y_, 0, c), NZ)]
        send(ref, ref, sib_sem.at[a, y_], sib)

    order = [zh] + zhs
    hops = (NY // 2, NY // 2 - 1)

    def ring_first(a, i):
        v = order[i]
        if i:
            ref = gbuf.at[a, block(y, v, c)]
            arrive(ref, zg_sem.at[a, v])
        hop(a, 0, 0, y, v)
        hop(a, 1, 0, y, v)
        if i == NZ - 1:
            to_sib(a, y)

    def ring_step(a, s):
        for i in range(NZ):
            v = order[i]
            for d in range(2):
                if s <= hops[d]:
                    y_ = ring(y - s * sg if d == 0 else y + s * sg, NY)
                    arrive(gbuf.at[a, block(y_, v, c)], y_sem.at[a, d, s - 1, v])
                    if s < hops[d]:
                        hop(a, d, s, y_, v)
                    if i == NZ - 1:
                        to_sib(a, y_)

    def ring_end(a):
        for y_ in range(NY):
            arrive(gbuf.at[a, pl.ds(block(y_, 0, other), NZ)], sib_sem.at[a, y_])

    merge(0)
    ring_first(0, 0)
    merge(1)
    ring_first(0, 1)
    ring_first(0, 2)

    for cp in loads:
        cp.wait()
    for i in range(2):
        parts = []
        for k in range(NL):
            v = wwin[i, k].astype(f32)
            turned = pltpu.roll(v, WIN - DP % 128, 1)
            parts.append(jnp.where(odd == 1, turned, v)[:, :DP])
        wsel[i] = jnp.concatenate(parts, axis=1).astype(bf16)

    ring_step(0, 1)

    for v in xs:
        arrive(prebuf.at[v], pre_sem.at[v])
    prebuf[pl.ds(x, 1)] = pre_ref[...][None]

    def pre_rows(q, carry):
        i = lax.broadcasted_iota(jnp.int32, (QR, QR), 0)
        j = lax.broadcasted_iota(jnp.int32, (QR, QR), 1)
        yz = QB * lax.rem(q, NX // NC) + (i >> 4)
        src = (yz * NC + q // (NX // NC)) * ROWS + (i & 3)
        total = jnp.zeros((QR, HID), f32)
        for p in range(NX):
            hot = jnp.where((src == j) & (((i >> 2) & 3) == p), 1.0, 0.0).astype(bf16)
            total += jnp.dot(hot, prebuf[p], preferred_element_type=f32)
        pref[q] = total
        act[q] = gelu_value(total).astype(bf16)
        return carry

    lax.fori_loop(0, NX, pre_rows, 0)

    ring_step(0, 2)
    ring_step(0, 3)
    ring_step(0, 4)
    ring_end(0)

    def rows_of(a, q):
        return gbuf[a, pl.ds(QB * q, QB)].reshape(QR, DQ)

    for v in xs + [x]:
        part = lax.dot_general(
            rows_of(0, v), wsel[0], (((1,), (1,)), ((), ())), preferred_element_type=f32
        )
        if v is x:
            gaown[...] = part
        else:
            pbuf[pl.ds(v, 1)] = part.astype(bf16)[None]
            send(pbuf.at[v], rsbuf.at[x], rs_sem.at[x], at(x_=v))
    for i in range(NZ):
        ring_first(1, i)

    scale_back = 1.0 / math.sqrt(NL * NX * NC * NB * ROWS)

    def weight_part(a, left):
        lhs = left[...].reshape(NX * QR, HID)
        for h in range(2):
            cols = 2 * DP
            right = gbuf[a, :, :, h * cols : (h + 1) * cols].reshape(NX * QR, cols)
            part = (
                lax.dot_general(lhs, right, (((0,), (0,)), ((), ())), preferred_element_type=f32)
                * scale_back
            ).astype(bf16)
            wchunk[a, 2 * h] = part[:, :DP]
            wchunk[a, 2 * h + 1] = part[:, DP:]
        for v in zls:
            send(wchunk.at[a, v], wrecv.at[a, zl], wr_sem.at[a, zl], at(zl_=v))

    def weight_sum(a, out):
        total = wchunk[a, pl.ds(zl, 1)][0].astype(f32)
        for v in zls:
            arrive(wrecv.at[a, v], wr_sem.at[a, v])
            total += wrecv[a, pl.ds(v, 1)][0].astype(f32)
        out[...] = total.astype(bf16)

    weight_part(0, act)
    ring_step(1, 1)

    total = gaown[...]
    for v in xs:
        arrive(rsbuf.at[v], rs_sem.at[v])
        total += rsbuf[pl.ds(v, 1)][0].astype(f32)
    grad_pre = (total * gelu_slope(pref[pl.ds(x, 1)][0])).astype(bf16)
    gpbuf[pl.ds(x, 1)] = grad_pre[None]
    for v in xs:
        send(gpbuf.at[x], gpbuf.at[x], ag_sem.at[x], at(x_=v))

    ring_step(1, 2)
    ring_step(1, 3)
    ring_step(1, 4)

    for v in xs:
        arrive(gpbuf.at[v], ag_sem.at[v])

    def in_part(first, keep):
        for h in range(2):
            part = jnp.dot(
                gpbuf[pl.ds(first * 2 + h, 1)][0], wsel[1], preferred_element_type=f32
            ).reshape(QB, BLK, DQ)
            if keep:
                gown[h * QB : (h + 1) * QB] = part
            else:
                gsend[h * QB : (h + 1) * QB] = part.astype(bf16)
                half = pl.ds(h * QB, QB)
                send(gsend.at[half], grecv.at[half], gs_sem.at[h], sib)

    in_part(other, False)
    in_part(c, True)
    for h in range(2):
        half = pl.ds(h * QB, QB)
        arrive(grecv.at[half], gs_sem.at[h])

    def own_sum(y_, zh_):
        b = y_ * NZ + zh_
        return gown[pl.ds(b, 1)][0] + grecv[pl.ds(b, 1)][0].astype(f32)

    for s in range(1, hops[0] + 1):
        for v in order:
            for d in range(2):
                if s <= hops[d]:
                    far = hops[d] + 1 - s
                    val = own_sum(ring(y + far * sg if d == 0 else y - far * sg, NY), v)
                    if s > 1:
                        arrive(rrecv.at[d, s - 2, v], ry_sem.at[d, s - 2, v])
                        val += rrecv[d, s - 2, pl.ds(v, 1)][0].astype(f32)
                    rsend[d, s - 1, pl.ds(v, 1)] = val.astype(bf16)[None]
                    send(
                        rsend.at[d, s - 1, v], rrecv.at[d, s - 1, v], ry_sem.at[d, s - 1, v],
                        fwd if d == 0 else bwd,
                    )
    for v in zhs + [zh]:
        val = own_sum(y, v)
        for d in range(2):
            s = hops[d] - 1
            arrive(rrecv.at[d, s, v], ry_sem.at[d, s, v])
            val += rrecv[d, s, pl.ds(v, 1)][0].astype(f32)
        if v is zh:
            zown[...] = val
        else:
            zsend[pl.ds(v, 1)] = val.astype(bf16)[None]
            send(zsend.at[v], zrecv.at[zh], rz_sem.at[zh], at(zh_=v))

    ring_end(1)
    weight_part(1, gpbuf)

    val = zown[...]
    for v in zhs:
        arrive(zrecv.at[v], rz_sem.at[v])
        val += zrecv[pl.ds(v, 1)][0].astype(f32)
    fbuf[...] = val
    for p in range(NX):
        osrc[p] = fbuf[ROWS * p : ROWS * (p + 1)].astype(bf16)
    for v in xs:
        send(osrc.at[v], obuf.at[x], ro_sem.at[x], at(x_=v))
    obuf[pl.ds(x, 1)] = osrc[pl.ds(x, 1)]

    weight_sum(0, gwo_ref)

    for v in xs:
        arrive(obuf.at[v], ro_sem.at[v])
    pieces = [obuf[p].astype(f32) for p in range(NX)]
    gin_ref[...] = jnp.concatenate(
        [pieces[p][:, k * DP : (k + 1) * DP] for k in range(NL) for p in range(NX)], axis=1
    ).astype(bf16)

    weight_sum(1, gwi_ref)

    for cp in flying:
        cp.wait_send()


def shards(tokens_in, grad_out, pre_act, w_in, w_out):
    vmem = pl.BlockSpec(memory_space=pltpu.VMEM)
    hbm = pl.BlockSpec(memory_space=pl.ANY)
    dma = pltpu.SemaphoreType.DMA
    grad_in, gwi, gwo = pl.pallas_call(
        kernel,
        out_shape=(
            jax.ShapeDtypeStruct((ROWS, WIDE), bf16),
            jax.ShapeDtypeStruct((HID, DP), bf16),
            jax.ShapeDtypeStruct((HID, DP), bf16),
        ),
        in_specs=[vmem, vmem, vmem, hbm, hbm],
        out_specs=(vmem, vmem, vmem),
        scratch_shapes=[
            pltpu.VMEM((2, NX, ROWS, DQ), bf16),
            pltpu.VMEM((2, NX, ROWS, DQ), bf16),
            pltpu.VMEM((BLK, DQ), f32),
            pltpu.VMEM((2, NBLK, BLK, DQ), bf16),
            pltpu.VMEM((2, NL, HID, WIN), bf16),
            pltpu.VMEM((2, HID, DQ), bf16),
            pltpu.VMEM((NX, QR, HID), bf16),
            pltpu.VMEM((NX, QR, HID), f32),
            pltpu.VMEM((NX, QR, HID), bf16),
            pltpu.VMEM((NX, QR, HID), bf16),
            pltpu.VMEM((QR, HID), f32),
            pltpu.VMEM((NX, QR, HID), bf16),
            pltpu.VMEM((NX, QR, HID), bf16),
            pltpu.VMEM((2, NL, HID, DP), bf16),
            pltpu.VMEM((2, NL, HID, DP), bf16),
            pltpu.VMEM((NB, BLK, DQ), f32),
            pltpu.VMEM((NB, BLK, DQ), bf16),
            pltpu.VMEM((NB, BLK, DQ), bf16),
            pltpu.VMEM((2, NY // 2, NZ, BLK, DQ), bf16),
            pltpu.VMEM((2, NY // 2, NZ, BLK, DQ), bf16),
            pltpu.VMEM((BLK, DQ), f32),
            pltpu.VMEM((NZ, BLK, DQ), bf16),
            pltpu.VMEM((NZ, BLK, DQ), bf16),
            pltpu.VMEM((BLK, DQ), f32),
            pltpu.VMEM((NX, ROWS, DQ), bf16),
            pltpu.VMEM((NX, ROWS, DQ), bf16),
            dma((160,)),
            dma((2, NX)),
            dma((NX,)),
            dma((2, NZ)),
            dma((2, 2, NY // 2, NZ)),
            dma((2, NY)),
            dma((2, NL)),
            dma((NX,)),
            dma((NX,)),
            dma((2, NL)),
            dma((2,)),
            dma((2, NY // 2, NZ)),
            dma((NZ,)),
            dma((NX,)),
        ],
        compiler_params=pltpu.CompilerParams(
            collective_id=0, has_side_effects=True, vmem_limit_bytes=48 * 1024 * 1024
        ),
        cost_estimate=pl.CostEstimate(
            flops=8 * 192 * 288 * 5120, bytes_accessed=4 * 1024 * 1024, transcendentals=0
        ),
        name="ffn_backward",
    )(grad_out, tokens_in, pre_act, w_out, w_in.T)
    return grad_in, gwi.T, gwo


def solution(mesh):
    placed = (
        P(("tokens", "mp"), None),
        P(("tokens", "mp"), None),
        P("tokens", "mp"),
        P(None, "mp"),
        P("mp", None),
    )
    return jax.shard_map(
        shards,
        mesh=mesh,
        in_specs=placed,
        out_specs=(P(("tokens", "mp"), None), P("tokens", "mp"), P("mp", "tokens")),
        check_vma=False,
    )
```

```python
import math

import jax
import jax.numpy as jnp
from jax import lax
from jax.experimental import pallas as pl
from jax.experimental.pallas import tpu as pltpu
from jax.sharding import PartitionSpec as P

root_two_pi = math.sqrt(2.0 / math.pi)
cubic = 0.044715

NY, NZ, NC = 8, 3, 2
NL, NX = 4, 4
ROWS = 4
BLK = ROWS * NX
NB = NY * NZ
NBLK = NC * NB
QR = NBLK * ROWS
GRP = NBLK // 4
GR = GRP * ROWS
NW = 4
WIDE = 5120
HID = 288
DQ = WIDE // NX
DP = DQ // NL
WIN = 384
MESH = pl.DeviceIdType.MESH
f32 = jnp.float32
bf16 = jnp.bfloat16


def gelu_value(pre):
    inner = root_two_pi * (pre + cubic * pre * pre * pre)
    return 0.5 * pre * (1.0 + jnp.tanh(inner))


def gelu_slope(pre):
    tanh_val = jnp.tanh(root_two_pi * (pre + cubic * pre * pre * pre))
    return 0.5 * (1.0 + tanh_val) + 0.5 * pre * (1.0 - tanh_val * tanh_val) * root_two_pi * (
        1.0 + 3.0 * cubic * pre * pre
    )


def kernel(
    go_ref, ti_ref, pre_ref, wo_ref, wi_ref,
    gin_ref, gwi_ref, gwo_ref,
    rows_in, xsrc, xbuf, mbuf, gbuf, sel, prebuf, wo, wi, slope, act, gpbuf, cgo, cti, gw,
    wchunk, wpair, wfar, wlast, gflat, gfold, grecv, rsend, rrecv, zown, zsend, zrecv,
    send_sem, in_sem, w_sem, x_sem, zg_sem, y_sem, sib_sem, act_sem, ag_sem, gw_sem, gwl_sem, gwsib_sem,
    wp_sem, wl_sem, gs_sem, ry_sem, rz_sem,
):
    m = lax.axis_index("mp")
    t = lax.axis_index("tokens")
    c = lax.rem(m, NC)
    zh = lax.rem(m // NC, NZ)
    y = m // (NC * NZ)
    x = lax.rem(t, NX)
    zl = t // NX
    sg = 1 - 2 * c

    def at(y_=None, zh_=None, c_=None, zl_=None, x_=None):
        y_ = y if y_ is None else y_
        zh_ = zh if zh_ is None else zh_
        c_ = c if c_ is None else c_
        zl_ = zl if zl_ is None else zl_
        x_ = x if x_ is None else x_
        return {"mp": (y_ * NZ + zh_) * NC + c_, "tokens": zl_ * NX + x_}

    def ring(v, n):
        return lax.rem(v + n, n)

    other = 1 - c
    xs = [lax.rem(x + d, NX) for d in range(1, NX)]
    zhs = [lax.rem(zh + d, NZ) for d in range(1, NZ)]
    near = zl + 1 - 2 * lax.rem(zl, 2)
    far_zl = lax.rem(zl + 2, NL)
    far_near = lax.rem(near + 2, NL)
    fwd = at(y_=ring(y + sg, NY))
    bwd = at(y_=ring(y - sg, NY))
    sib = at(c_=other)
    flying = []

    def send(src, dst, sem, dev):
        cp = pltpu.make_async_remote_copy(
            src_ref=src, dst_ref=dst, send_sem=send_sem.at[len(flying)], recv_sem=sem,
            device_id=dev, device_id_type=MESH,
        )
        cp.start()
        flying.append(cp)

    def arrive(dst, sem):
        pltpu.make_async_remote_copy(
            src_ref=dst, dst_ref=dst, send_sem=send_sem.at[0], recv_sem=sem,
            device_id=sib, device_id_type=MESH,
        ).wait_recv()

    first = [
        pltpu.make_async_copy(go_ref, rows_in.at[0], in_sem.at[0]),
        pltpu.make_async_copy(ti_ref, rows_in.at[1], in_sem.at[1]),
        pltpu.make_async_copy(pre_ref, prebuf, in_sem.at[2]),
    ]
    for cp in first:
        cp.start()

    barrier = pltpu.get_barrier_semaphore()
    peers = (
        [at(x_=v) for v in xs] + [at(zh_=v) for v in zhs] + [at(zl_=near), at(zl_=far_zl)]
        + [fwd, bwd, sib]
    )
    for dev in peers:
        pl.semaphore_signal(barrier, inc=1, device_id=dev, device_id_type=MESH)

    loads = [
        pltpu.make_async_copy(wo_ref, wo, w_sem.at[0]),
        pltpu.make_async_copy(wi_ref, wi, w_sem.at[1]),
    ]
    for cp in loads:
        cp.start()

    def block(y_, zh_, c_):
        return c_ * NB + y_ * NZ + zh_

    first[0].wait()
    v = rows_in[0].astype(f32)
    for n in range(NW):
        mbuf[ROWS * n : ROWS * (n + 1)] = v[:, n * DQ : (n + 1) * DQ]
    gbuf[0, pl.ds(block(y, zh, c), 1)] = mbuf[...].astype(bf16)[None]
    first[1].wait()
    v = rows_in[1].astype(f32)
    for p in range(NX):
        xsrc[p] = jnp.concatenate(
            [v[:, k * DQ + p * DP : k * DQ + (p + 1) * DP] for k in range(NL)], axis=1
        ).astype(bf16)

    pl.semaphore_wait(barrier, len(peers))

    def spread(a):
        mine = gbuf.at[a, block(y, zh, c)]
        for v in zhs:
            send(mine, mine, zg_sem.at[a, zh], at(zh_=v))

    def hop(a, d, s, y_, zh_):
        ref = gbuf.at[a, block(y_, zh_, c)]
        send(ref, ref, y_sem.at[a, d, s, zh_], fwd if d == 0 else bwd)

    def to_sib(a, y_):
        ref = gbuf.at[a, pl.ds(block(y_, 0, c), NZ)]
        send(ref, ref, sib_sem.at[a, y_], sib)

    order = [zh] + zhs
    hops = (NY // 2, NY // 2 - 1)

    def ring_first(a, i):
        v = order[i]
        if i:
            ref = gbuf.at[a, block(y, v, c)]
            arrive(ref, zg_sem.at[a, v])
        hop(a, 0, 0, y, v)
        hop(a, 1, 0, y, v)
        if i == NZ - 1:
            to_sib(a, y)

    def ring_step(a, s):
        for i in range(NZ):
            v = order[i]
            for d in range(2):
                if s <= hops[d]:
                    y_ = ring(y - s * sg if d == 0 else y + s * sg, NY)
                    arrive(gbuf.at[a, block(y_, v, c)], y_sem.at[a, d, s - 1, v])
                    if s < hops[d]:
                        hop(a, d, s, y_, v)
                    if i == NZ - 1:
                        to_sib(a, y_)

    spread(0)
    ring_first(0, 0)
    for v in xs:
        send(xsrc.at[v], xbuf.at[x], x_sem.at[x], at(x_=v))
    xbuf[pl.ds(x, 1)] = xsrc[pl.ds(x, 1)]

    pairs = [(y, ring(y + 4, NY))] + [(ring(y + g, NY), ring(y - g, NY)) for g in range(1, 4)]
    i = lax.broadcasted_iota(jnp.int32, (QR, QR), 0)
    j = lax.broadcasted_iota(jnp.int32, (QR, QR), 1)

    n = (i >= GR).astype(jnp.int32) + (i >= 2 * GR).astype(jnp.int32) + (i >= 3 * GR).astype(jnp.int32)
    sel[...] = jnp.where(((i >> 2) - GRP * n) * BLK + n * ROWS + (i & 3) == j, 1.0, 0.0).astype(bf16)

    first[2].wait()
    q = (i * 43691) >> 19
    rest = i - 12 * q
    g = q >> 2
    ahead = jnp.where((q & 2) == 0, g, jnp.where(g == 0, 4, NY - g))
    src = ((y + ahead) & (NY - 1)) * (NZ * NC * ROWS) + (rest >> 2) * (NC * ROWS) + (q & 1) * ROWS + (rest & 3)
    hot = jnp.where(src == j, 1.0, 0.0).astype(bf16)
    pre = jnp.dot(hot, prebuf[...], preferred_element_type=f32)
    slope[...] = gelu_slope(pre)
    act[pl.ds(x, 1)] = gelu_value(pre).astype(bf16)[None]
    for v in xs:
        send(act.at[x], act.at[x], act_sem.at[x], at(x_=v))

    ring_first(0, 1)
    ring_first(0, 2)

    for v in xs:
        arrive(xbuf.at[v], x_sem.at[v])
    for p in range(NX):
        mbuf[ROWS * p : ROWS * (p + 1)] = xbuf[p].astype(f32)
    gbuf[1, pl.ds(block(y, zh, c), 1)] = mbuf[...].astype(bf16)[None]
    spread(1)

    def group(a, g):
        for y_ in pairs[g]:
            arrive(gbuf.at[a, pl.ds(block(y_, 0, other), NZ)], sib_sem.at[a, y_])
        rows = [gbuf[a, pl.ds(block(y_, 0, c_), NZ)] for y_ in pairs[g] for c_ in range(NC)]
        return jnp.dot(
            sel[...], jnp.concatenate(rows, axis=0).reshape(QR, DQ), preferred_element_type=f32
        ).astype(bf16)

    def window(v, n):
        low = pl.multiple_of(((v * DP) // 128) * 128, 128)
        return pl.ds(pl.multiple_of(low + n * DQ, 128), WIN)

    def out_group(g):
        part = group(0, g)
        rows = slice(g * GR, (g + 1) * GR)
        for n in range(NW):
            cgo[rows, n * DQ : (n + 1) * DQ] = part[n * GR : (n + 1) * GR]
        for v in xs:
            for k in range(2):
                n = 2 * c + k
                send(
                    cgo.at[rows, window(v, n)], gw.at[n, x, rows], gw_sem.at[x, g, k], at(x_=v)
                )

    def pass_on(g):
        rows = slice(g * GR, (g + 1) * GR)
        for v in xs:
            for k in range(2):
                arrive(gw.at[2 * c + k, v, rows], gw_sem.at[v, g, k])
            mine = gw.at[pl.ds(2 * c, 2), v, rows]
            send(mine, mine, gwsib_sem.at[v, g], sib)

    ring_step(0, 1)
    ring_step(0, 2)
    out_group(1)
    ring_step(0, 3)
    out_group(2)
    ring_step(0, 4)
    for i in range(NZ):
        ring_first(1, i)
    out_group(3)
    out_group(0)
    pass_on(1)
    pass_on(2)
    own = [
        pltpu.make_async_copy(cgo.at[:, window(x, n)], gw.at[n, x], gwl_sem.at[n]) for n in range(NW)
    ]
    for cp in own:
        cp.start()

    for cp in loads:
        cp.wait()
    grad_act = lax.dot_general(
        cgo[...], wo[...], (((1,), (1,)), ((), ())), preferred_element_type=f32
    )
    gpbuf[pl.ds(x, 1)] = (grad_act * slope[...]).astype(bf16)[None]
    for v in xs:
        send(gpbuf.at[x], gpbuf.at[x], ag_sem.at[x], at(x_=v))

    ring_step(1, 1)

    grad_pre = gpbuf[pl.ds(x, 1)][0]
    for n in range(NW):
        part = jnp.dot(grad_pre, wi[:, n * DQ : (n + 1) * DQ], preferred_element_type=f32)
        gflat[n] = part.astype(bf16)
    for g in range(4):
        rows = gflat[:, g * GR : (g + 1) * GR, :].reshape(QR, DQ)
        part = lax.dot_general(
            sel[...], rows, (((0,), (0,)), ((), ())), preferred_element_type=f32
        ).astype(bf16).reshape(GRP, BLK, DQ)
        k = 0
        for y_ in pairs[g]:
            for c_ in range(NC):
                gfold[c_, pl.ds(y_ * NZ, NZ)] = part[k : k + NZ]
                k += NZ
    for h in range(2):
        some = pl.ds(h * (NB // 2), NB // 2)
        send(gfold.at[other, some], grecv.at[some], gs_sem.at[h], sib)

    ring_step(1, 2)
    pass_on(3)
    pass_on(0)

    for h in range(2):
        some = pl.ds(h * (NB // 2), NB // 2)
        arrive(grecv.at[some], gs_sem.at[h])

    def own_sum(y_, zh_):
        b = y_ * NZ + zh_
        return gfold[c, pl.ds(b, 1)][0].astype(f32) + grecv[pl.ds(b, 1)][0].astype(f32)

    def sum_step(s):
        for v in order:
            for d in range(2):
                if s <= hops[d]:
                    far = hops[d] + 1 - s
                    val = own_sum(ring(y + far * sg if d == 0 else y - far * sg, NY), v)
                    if s > 1:
                        arrive(rrecv.at[d, s - 2, v], ry_sem.at[d, s - 2, v])
                        val += rrecv[d, s - 2, pl.ds(v, 1)][0].astype(f32)
                    rsend[d, s - 1, pl.ds(v, 1)] = val.astype(bf16)[None]
                    send(
                        rsend.at[d, s - 1, v], rrecv.at[d, s - 1, v], ry_sem.at[d, s - 1, v],
                        fwd if d == 0 else bwd,
                    )

    scale_back = 1.0 / math.sqrt(NL * NX * NC * NB * ROWS)
    odd = lax.rem(x, 2)

    def weight_part(lhs, right):
        return (
            lax.dot_general(lhs, right, (((0,), (0,)), ((), ())), preferred_element_type=f32)
            * scale_back
        )

    def put_chunk(a, k, piece):
        wchunk[a, k] = jnp.concatenate([piece[: HID // 2], piece[HID // 2 :]], axis=1).astype(bf16)

    def weight_pair(a):
        dev = at(zl_=near)
        send(wchunk.at[a, far_near], wpair.at[a, 1], wp_sem.at[a, 1], dev)
        send(wchunk.at[a, near], wpair.at[a, 0], wp_sem.at[a, 0], dev)

    def weight_far(a):
        arrive(wpair.at[a, 1], wp_sem.at[a, 1])
        val = wchunk[a, pl.ds(far_zl, 1)][0].astype(f32) + wpair[a, 1].astype(f32)
        wfar[a] = val.astype(bf16)
        send(wfar.at[a], wlast.at[a], wl_sem.at[a], at(zl_=far_zl))

    def weight_sum(a, out):
        arrive(wpair.at[a, 0], wp_sem.at[a, 0])
        arrive(wlast.at[a], wl_sem.at[a])
        val = wchunk[a, pl.ds(zl, 1)][0].astype(f32)
        val = (val + wpair[a, 0].astype(f32) + wlast[a].astype(f32)).astype(bf16)
        out[: HID // 2] = val[:, :DP]
        out[HID // 2 :] = val[:, DP:]

    sum_step(1)
    ring_step(1, 3)

    for cp in own:
        cp.wait()
    for v in xs:
        arrive(act.at[v], act_sem.at[v])
        for g in range(4):
            arrive(gw.at[pl.ds(2 * other, 2), v, slice(g * GR, (g + 1) * GR)], gwsib_sem.at[v, g])
    left = act[...].reshape(NX * QR, HID)
    for n in range(NW):
        part = weight_part(left, gw[n].reshape(NX * QR, WIN))
        turned = pltpu.roll(part, WIN - DP % 128, 1)
        put_chunk(0, n, jnp.where(odd == 1, turned, part)[:, :DP])
    weight_pair(0)

    sum_step(2)
    ring_step(1, 4)
    for g in (1, 2, 3, 0):
        part = group(1, g)
        for p in range(NX):
            cti[p * QR + g * GR : p * QR + (g + 1) * GR] = part[p * GR : (p + 1) * GR]
        if g == 2:
            sum_step(3)

    for v in xs:
        arrive(gpbuf.at[v], ag_sem.at[v])
    left = gpbuf[...].reshape(NX * QR, HID)
    for h in range(2):
        part = weight_part(left, cti[:, 2 * h * DP : 2 * (h + 1) * DP])
        for k in range(2):
            put_chunk(1, 2 * h + k, part[:, k * DP : (k + 1) * DP])
        if h == 0:
            sum_step(4)
    weight_pair(1)
    weight_far(0)

    for i, v in enumerate(zhs + [zh]):
        val = own_sum(y, v)
        for d in range(2):
            s = hops[d] - 1
            arrive(rrecv.at[d, s, v], ry_sem.at[d, s, v])
            val += rrecv[d, s, pl.ds(v, 1)][0].astype(f32)
        if i == NZ - 1:
            zown[...] = val
        else:
            zsend[pl.ds(v, 1)] = val.astype(bf16)[None]
            send(zsend.at[v], zrecv.at[zh], rz_sem.at[zh], at(zh_=v))

    weight_far(1)

    val = zown[...]
    for v in zhs:
        arrive(zrecv.at[v], rz_sem.at[v])
        val += zrecv[pl.ds(v, 1)][0].astype(f32)
    for n in range(NW):
        gin_ref[:, n * DQ : (n + 1) * DQ] = val[ROWS * n : ROWS * (n + 1)].astype(bf16)

    weight_sum(0, gwo_ref)
    weight_sum(1, gwi_ref)

    for cp in flying:
        cp.wait_send()


def deliver(a_ref, b_ref, d_ref, a_out, b_out, d_out):
    a_out[...] = a_ref[...]
    b_out[...] = b_ref[...]
    d_out[...] = d_ref[...]


def shards(tokens_in, grad_out, pre_act, w_in, w_out):
    vmem = pl.BlockSpec(memory_space=pltpu.VMEM)
    hbm = pl.BlockSpec(memory_space=pltpu.HBM)
    dma = pltpu.SemaphoreType.DMA
    shapes = (
        jax.ShapeDtypeStruct((ROWS, WIDE), bf16),
        jax.ShapeDtypeStruct((HID, DP), bf16),
        jax.ShapeDtypeStruct((HID, DP), bf16),
    )
    outs = pl.pallas_call(
        kernel,
        out_shape=shapes,
        in_specs=[hbm] * 5,
        out_specs=(vmem, vmem, vmem),
        scratch_shapes=[
            pltpu.VMEM((2, ROWS, WIDE), bf16),
            pltpu.VMEM((NX, ROWS, DQ), bf16),
            pltpu.VMEM((NX, ROWS, DQ), bf16),
            pltpu.VMEM((BLK, DQ), f32),
            pltpu.VMEM((2, NBLK, BLK, DQ), bf16),
            pltpu.VMEM((QR, QR), bf16),
            pltpu.VMEM((QR, HID), bf16),
            pltpu.VMEM((HID, WIDE), bf16),
            pltpu.VMEM((HID, WIDE), bf16),
            pltpu.VMEM((QR, HID), f32),
            pltpu.VMEM((NX, QR, HID), bf16),
            pltpu.VMEM((NX, QR, HID), bf16),
            pltpu.VMEM((QR, WIDE), bf16),
            pltpu.VMEM((NX * QR, DQ), bf16),
            pltpu.VMEM((NW, NX, QR, WIN), bf16),
            pltpu.VMEM((2, NL, HID // 2, 2 * DP), bf16),
            pltpu.VMEM((2, 2, HID // 2, 2 * DP), bf16),
            pltpu.VMEM((2, HID // 2, 2 * DP), bf16),
            pltpu.VMEM((2, HID // 2, 2 * DP), bf16),
            pltpu.VMEM((NW, QR, DQ), bf16),
            pltpu.VMEM((NC, NB, BLK, DQ), bf16),
            pltpu.VMEM((NB, BLK, DQ), bf16),
            pltpu.VMEM((2, NY // 2, NZ, BLK, DQ), bf16),
            pltpu.VMEM((2, NY // 2, NZ, BLK, DQ), bf16),
            pltpu.VMEM((BLK, DQ), f32),
            pltpu.VMEM((NZ, BLK, DQ), bf16),
            pltpu.VMEM((NZ, BLK, DQ), bf16),
            dma((200,)),
            dma((3,)),
            dma((2,)),
            dma((NX,)),
            dma((2, NZ)),
            dma((2, 2, NY // 2, NZ)),
            dma((2, NY)),
            dma((NX,)),
            dma((NX,)),
            dma((NX, 4, 2)),
            dma((NW,)),
            dma((NX, 4)),
            dma((2, 2)),
            dma((2,)),
            dma((2,)),
            dma((2, NY // 2, NZ)),
            dma((NZ,)),
        ],
        compiler_params=pltpu.CompilerParams(
            collective_id=0, has_side_effects=True, vmem_limit_bytes=60 * 1024 * 1024
        ),
        cost_estimate=pl.CostEstimate(
            flops=8 * 192 * 288 * 5120, bytes_accessed=4 * 1024 * 1024, transcendentals=0
        ),
        name="ffn_backward",
    )(grad_out, tokens_in, pre_act, w_out, w_in.T)
    grad_in, gwi, gwo = pl.pallas_call(
        deliver,
        out_shape=shapes,
        in_specs=[vmem] * 3,
        out_specs=(vmem,) * 3,
        compiler_params=pltpu.CompilerParams(vmem_limit_bytes=60 * 1024 * 1024),
        name="deliver",
    )(*outs)
    return grad_in, gwi.T, gwo


def solution(mesh):
    placed = (
        P(("tokens", "mp"), None),
        P(("tokens", "mp"), None),
        P("tokens", "mp"),
        P(None, "mp"),
        P("mp", None),
    )
    return jax.shard_map(
        shards,
        mesh=mesh,
        in_specs=placed,
        out_specs=(P(("tokens", "mp"), None), P("tokens", "mp"), P("mp", "tokens")),
        check_vma=False,
    )
```

```python
import math

import jax
import jax.numpy as jnp
from jax import lax
from jax.experimental import pallas as pl
from jax.experimental.pallas import tpu as pltpu
from jax.sharding import PartitionSpec as P

root_two_pi = math.sqrt(2.0 / math.pi)
cubic = 0.044715

NY, NZ, NC = 8, 3, 2
NL, NX = 4, 4
ROWS = 4
BLK = ROWS * NX
NB = NY * NZ
NBLK = NC * NB
QR = NBLK * ROWS
GRP = NBLK // 4
GR = GRP * ROWS
NW = 4
WIDE = 5120
HID = 288
DQ = WIDE // NX
DP = DQ // NL
NH = NZ * NL
HQ = DQ // NC
MESH = pl.DeviceIdType.MESH
f32 = jnp.float32
bf16 = jnp.bfloat16


def gelu_value(pre):
    inner = root_two_pi * (pre + cubic * pre * pre * pre)
    return 0.5 * pre * (1.0 + jnp.tanh(inner))


def gelu_slope(pre):
    tanh_val = jnp.tanh(root_two_pi * (pre + cubic * pre * pre * pre))
    return 0.5 * (1.0 + tanh_val) + 0.5 * pre * (1.0 - tanh_val * tanh_val) * root_two_pi * (
        1.0 + 3.0 * cubic * pre * pre
    )


def kernel(
    go_ref, ti_ref, pre_ref, wo_ref, wi_ref,
    gin_ref, gwi_ref, gwo_ref,
    rows_in, xsrc, xbuf, mbuf, gbuf, sel, prebuf, wo, wi, slope, act, gpbuf, cgo, cti, gw,
    wchunk, wpair, wfar, wlast, wx, gflat, gfold, grecv, rsend, rrecv, zown, zsend, zrecv,
    send_sem, in_sem, w_sem, x_sem, zg_sem, y_sem, sib_sem, act_sem, ag_sem, gw_sem, gwl_sem, gwsib_sem,
    wp_sem, wl_sem, wx_sem, gs_sem, ry_sem, rz_sem,
):
    m = lax.axis_index("mp")
    t = lax.axis_index("tokens")
    c = lax.rem(m, NC)
    zh = lax.rem(m // NC, NZ)
    y = m // (NC * NZ)
    x = lax.rem(t, NX)
    zl = t // NX
    sg = 1 - 2 * c

    def at(y_=None, zh_=None, c_=None, zl_=None, x_=None):
        y_ = y if y_ is None else y_
        zh_ = zh if zh_ is None else zh_
        c_ = c if c_ is None else c_
        zl_ = zl if zl_ is None else zl_
        x_ = x if x_ is None else x_
        return {"mp": (y_ * NZ + zh_) * NC + c_, "tokens": zl_ * NX + x_}

    def ring(v, n):
        return lax.rem(v + n, n)

    other = 1 - c
    xs = [lax.rem(x + d, NX) for d in range(1, NX)]
    zhs = [lax.rem(zh + d, NZ) for d in range(1, NZ)]
    zls = [lax.rem(zl + d, NL) for d in range(1, NL)]
    z = zh * NL + zl

    def along(d):
        z_ = lax.rem(z + d + NH, NH)
        return at(zh_=z_ // NL, zl_=lax.rem(z_, NL))

    near = zl + 1 - 2 * lax.rem(zl, 2)
    far_zl = lax.rem(zl + 2, NL)
    far_near = lax.rem(near + 2, NL)
    fwd = at(y_=ring(y + sg, NY))
    bwd = at(y_=ring(y - sg, NY))
    sib = at(c_=other)
    flying = []

    def send(src, dst, sem, dev):
        cp = pltpu.make_async_remote_copy(
            src_ref=src, dst_ref=dst, send_sem=send_sem.at[len(flying)], recv_sem=sem,
            device_id=dev, device_id_type=MESH,
        )
        cp.start()
        flying.append(cp)

    def arrive(dst, sem):
        pltpu.make_async_remote_copy(
            src_ref=dst, dst_ref=dst, send_sem=send_sem.at[0], recv_sem=sem,
            device_id=sib, device_id_type=MESH,
        ).wait_recv()

    first = [
        pltpu.make_async_copy(go_ref, rows_in.at[0], in_sem.at[0]),
        pltpu.make_async_copy(ti_ref, rows_in.at[1], in_sem.at[1]),
        pltpu.make_async_copy(pre_ref, prebuf, in_sem.at[2]),
    ]
    for cp in first:
        cp.start()

    barrier = pltpu.get_barrier_semaphore()
    peers = (
        [at(x_=v) for v in xs] + [along(d) for d in (1, 2, 3, 4, -1, -2, -3, -4)]
        + [fwd, bwd, sib]
    )
    for dev in peers:
        pl.semaphore_signal(barrier, inc=1, device_id=dev, device_id_type=MESH)

    loads = [
        pltpu.make_async_copy(wo_ref, wo, w_sem.at[0]),
        pltpu.make_async_copy(wi_ref, wi, w_sem.at[1]),
    ]
    for cp in loads:
        cp.start()

    def block(y_, zh_, c_):
        return c_ * NB + y_ * NZ + zh_

    first[0].wait()
    v = rows_in[0].astype(f32)
    for n in range(NW):
        mbuf[ROWS * n : ROWS * (n + 1)] = v[:, n * DQ : (n + 1) * DQ]
    gbuf[0, pl.ds(block(y, zh, c), 1)] = mbuf[...].astype(bf16)[None]
    first[1].wait()
    v = rows_in[1].astype(f32)
    for p in range(NX):
        xsrc[p] = jnp.concatenate(
            [v[:, k * DQ + p * DP : k * DQ + (p + 1) * DP] for k in range(NL)], axis=1
        ).astype(bf16)

    pl.semaphore_wait(barrier, len(peers))

    def spread(a):
        mine = gbuf.at[a, block(y, zh, c)]
        for v in zhs:
            send(mine, mine, zg_sem.at[a, zh], at(zh_=v))

    def hop(a, d, s, y_, zh_):
        ref = gbuf.at[a, block(y_, zh_, c)]
        send(ref, ref, y_sem.at[a, d, s, zh_], fwd if d == 0 else bwd)

    def to_sib(a, y_):
        ref = gbuf.at[a, pl.ds(block(y_, 0, c), NZ)]
        send(ref, ref, sib_sem.at[a, y_], sib)

    order = [zh] + zhs
    hops = (NY // 2, NY // 2 - 1)

    def ring_first(a, i):
        v = order[i]
        if i:
            ref = gbuf.at[a, block(y, v, c)]
            arrive(ref, zg_sem.at[a, v])
        hop(a, 0, 0, y, v)
        hop(a, 1, 0, y, v)
        if i == NZ - 1:
            to_sib(a, y)

    def ring_step(a, s):
        for i in range(NZ):
            v = order[i]
            for d in range(2):
                if s <= hops[d]:
                    y_ = ring(y - s * sg if d == 0 else y + s * sg, NY)
                    arrive(gbuf.at[a, block(y_, v, c)], y_sem.at[a, d, s - 1, v])
                    if s < hops[d]:
                        hop(a, d, s, y_, v)
                    if i == NZ - 1:
                        to_sib(a, y_)

    spread(0)
    ring_first(0, 0)
    for v in xs:
        send(xsrc.at[v], xbuf.at[x], x_sem.at[x], at(x_=v))
    xbuf[pl.ds(x, 1)] = xsrc[pl.ds(x, 1)]

    pairs = [(y, ring(y + 4, NY))] + [(ring(y + g, NY), ring(y - g, NY)) for g in range(1, 4)]
    i = lax.broadcasted_iota(jnp.int32, (QR, QR), 0)
    j = lax.broadcasted_iota(jnp.int32, (QR, QR), 1)

    n = (i >= GR).astype(jnp.int32) + (i >= 2 * GR).astype(jnp.int32) + (i >= 3 * GR).astype(jnp.int32)
    sel[...] = jnp.where(((i >> 2) - GRP * n) * BLK + n * ROWS + (i & 3) == j, 1.0, 0.0).astype(bf16)

    first[2].wait()
    q = (i * 43691) >> 19
    rest = i - 12 * q
    g = q >> 2
    ahead = jnp.where((q & 2) == 0, g, jnp.where(g == 0, 4, NY - g))
    src = ((y + ahead) & (NY - 1)) * (NZ * NC * ROWS) + (rest >> 2) * (NC * ROWS) + (q & 1) * ROWS + (rest & 3)
    hot = jnp.where(src == j, 1.0, 0.0).astype(bf16)
    pre = jnp.dot(hot, prebuf[...], preferred_element_type=f32)
    slope[...] = gelu_slope(pre)
    act[pl.ds(zl, 1)] = gelu_value(pre).astype(bf16)[None]

    ring_first(0, 1)
    ring_first(0, 2)

    for v in xs:
        arrive(xbuf.at[v], x_sem.at[v])
    for p in range(NX):
        mbuf[ROWS * p : ROWS * (p + 1)] = xbuf[p].astype(f32)
    gbuf[1, pl.ds(block(y, zh, c), 1)] = mbuf[...].astype(bf16)[None]
    spread(1)
    for v in zls:
        send(act.at[zl], act.at[zl], act_sem.at[zl], at(zl_=v))

    def group(a, g):
        for y_ in pairs[g]:
            arrive(gbuf.at[a, pl.ds(block(y_, 0, other), NZ)], sib_sem.at[a, y_])
        rows = [gbuf[a, pl.ds(block(y_, 0, c_), NZ)] for y_ in pairs[g] for c_ in range(NC)]
        return jnp.dot(
            sel[...], jnp.concatenate(rows, axis=0).reshape(QR, DQ), preferred_element_type=f32
        ).astype(bf16)

    def out_group(g):
        part = group(0, g)
        rows = slice(g * GR, (g + 1) * GR)
        for n in range(NW):
            cgo[rows, n * DQ : (n + 1) * DQ] = part[n * GR : (n + 1) * GR]

    def out_send(g):
        rows = slice(g * GR, (g + 1) * GR)
        for v, d in zip(zls, (1, 2 * sg, -1)):
            send(
                cgo.at[rows, cols(v * DQ + c * HQ)], gw.at[zl, rows, cols(c * HQ)], gw_sem.at[zl, g], along(d)
            )

    def cols(low):
        return pl.ds(pl.multiple_of(low, 128), HQ)

    def pass_on(g):
        rows = slice(g * GR, (g + 1) * GR)
        for v in zls:
            mine = gw.at[v, rows, cols(c * HQ)]
            arrive(mine, gw_sem.at[v, g])
            send(mine, mine, gwsib_sem.at[v, g], sib)

    ring_step(0, 1)
    ring_step(0, 2)
    out_group(1)
    out_send(1)
    ring_step(0, 3)
    out_group(2)
    out_send(2)
    ring_step(0, 4)
    for i in range(NZ):
        ring_first(1, i)
    out_group(3)
    out_group(0)

    for cp in loads:
        cp.wait()
    grad_act = lax.dot_general(
        cgo[...], wo[...], (((1,), (1,)), ((), ())), preferred_element_type=f32
    )
    gpbuf[pl.ds(x, 1)] = (grad_act * slope[...]).astype(bf16)[None]
    for v in xs:
        send(gpbuf.at[x], gpbuf.at[x], ag_sem.at[x], at(x_=v))

    ring_step(1, 1)

    grad_pre = gpbuf[pl.ds(x, 1)][0]
    for n in range(NW):
        part = jnp.dot(grad_pre, wi[:, n * DQ : (n + 1) * DQ], preferred_element_type=f32)
        gflat[n] = part.astype(bf16)
    for g in range(4):
        rows = gflat[:, g * GR : (g + 1) * GR, :].reshape(QR, DQ)
        part = lax.dot_general(
            sel[...], rows, (((0,), (0,)), ((), ())), preferred_element_type=f32
        ).astype(bf16).reshape(GRP, BLK, DQ)
        k = 0
        for y_ in pairs[g]:
            for c_ in range(NC):
                gfold[c_, pl.ds(y_ * NZ, NZ)] = part[k : k + NZ]
                k += NZ
    for h in range(2):
        some = pl.ds(h * (NB // 2), NB // 2)
        send(gfold.at[other, some], grecv.at[some], gs_sem.at[h], sib)

    ring_step(1, 2)
    out_send(3)
    out_send(0)
    own = pltpu.make_async_copy(
        cgo.at[:, pl.ds(pl.multiple_of(zl * DQ, 128), DQ)], gw.at[zl], gwl_sem.at[0]
    )
    own.start()

    for h in range(2):
        some = pl.ds(h * (NB // 2), NB // 2)
        arrive(grecv.at[some], gs_sem.at[h])

    def own_sum(y_, zh_):
        b = y_ * NZ + zh_
        return gfold[c, pl.ds(b, 1)][0].astype(f32) + grecv[pl.ds(b, 1)][0].astype(f32)

    def sum_step(s):
        for v in order:
            for d in range(2):
                if s <= hops[d]:
                    far = hops[d] + 1 - s
                    val = own_sum(ring(y + far * sg if d == 0 else y - far * sg, NY), v)
                    if s > 1:
                        arrive(rrecv.at[d, s - 2, v], ry_sem.at[d, s - 2, v])
                        val += rrecv[d, s - 2, pl.ds(v, 1)][0].astype(f32)
                    rsend[d, s - 1, pl.ds(v, 1)] = val.astype(bf16)[None]
                    send(
                        rsend.at[d, s - 1, v], rrecv.at[d, s - 1, v], ry_sem.at[d, s - 1, v],
                        fwd if d == 0 else bwd,
                    )

    scale_back = 1.0 / math.sqrt(NL * NX * NC * NB * ROWS)

    def weight_parts(a, lhs, right):
        for h in range(2):
            some = slice(2 * h * DP, 2 * (h + 1) * DP)
            rows = right[..., some].reshape(NX * QR, 2 * DP)
            part = scale_back * lax.dot_general(
                lhs, rows, (((0,), (0,)), ((), ())), preferred_element_type=f32
            )
            for k in range(2):
                put_chunk(a, 2 * h + k, part[:, k * DP : (k + 1) * DP])

    def put_chunk(a, k, piece):
        wchunk[a, k] = jnp.concatenate([piece[: HID // 2], piece[HID // 2 :]], axis=1).astype(bf16)

    def weight_pair(a):
        dev = at(zl_=near)
        send(wchunk.at[a, far_near], wpair.at[1], wp_sem.at[1], dev)
        send(wchunk.at[a, near], wpair.at[0], wp_sem.at[0], dev)

    def weight_far(a):
        arrive(wpair.at[1], wp_sem.at[1])
        val = wchunk[a, pl.ds(far_zl, 1)][0].astype(f32) + wpair[1].astype(f32)
        wfar[...] = val.astype(bf16)
        send(wfar, wlast, wl_sem.at[0], at(zl_=far_zl))

    def put_sum(val, out):
        out[: HID // 2] = val[:, :DP].astype(bf16)
        out[HID // 2 :] = val[:, DP:].astype(bf16)

    def in_group(g):
        part = group(1, g)
        for p in range(NX):
            cti[p * QR + g * GR : p * QR + (g + 1) * GR] = part[p * GR : (p + 1) * GR]

    sum_step(1)
    ring_step(1, 3)
    in_group(1)
    sum_step(2)
    in_group(2)
    ring_step(1, 4)
    sum_step(3)
    in_group(3)
    in_group(0)

    for v in xs:
        arrive(gpbuf.at[v], ag_sem.at[v])
    weight_parts(1, gpbuf[...].reshape(NX * QR, HID), cti)
    weight_pair(1)
    pass_on(1)
    pass_on(2)
    sum_step(4)
    pass_on(3)
    pass_on(0)

    own.wait()
    for v in zls:
        arrive(act.at[v], act_sem.at[v])
        for g in range(4):
            arrive(gw.at[v, slice(g * GR, (g + 1) * GR), cols(other * HQ)], gwsib_sem.at[v, g])
    weight_parts(0, act[...].reshape(NX * QR, HID), gw)
    for v in xs:
        send(wchunk.at[0, v], wx.at[x], wx_sem.at[x], at(x_=v))

    weight_far(1)

    for i, v in enumerate(zhs + [zh]):
        val = own_sum(y, v)
        for d in range(2):
            s = hops[d] - 1
            arrive(rrecv.at[d, s, v], ry_sem.at[d, s, v])
            val += rrecv[d, s, pl.ds(v, 1)][0].astype(f32)
        if i == NZ - 1:
            zown[...] = val
        else:
            zsend[pl.ds(v, 1)] = val.astype(bf16)[None]
            send(zsend.at[v], zrecv.at[zh], rz_sem.at[zh], at(zh_=v))

    val = zown[...]
    for v in zhs:
        arrive(zrecv.at[v], rz_sem.at[v])
        val += zrecv[pl.ds(v, 1)][0].astype(f32)
    for n in range(NW):
        gin_ref[:, n * DQ : (n + 1) * DQ] = val[ROWS * n : ROWS * (n + 1)].astype(bf16)

    val = wchunk[0, pl.ds(x, 1)][0].astype(f32)
    for v in xs:
        arrive(wx.at[v], wx_sem.at[v])
        val += wx[pl.ds(v, 1)][0].astype(f32)
    put_sum(val, gwo_ref)

    arrive(wpair.at[0], wp_sem.at[0])
    val = wchunk[1, pl.ds(zl, 1)][0].astype(f32) + wpair[0].astype(f32)
    arrive(wlast, wl_sem.at[0])
    put_sum(val + wlast[...].astype(f32), gwi_ref)

    for cp in flying:
        cp.wait_send()


def deliver(a_ref, b_ref, d_ref, a_out, b_out, d_out):
    a_out[...] = a_ref[...]
    b_out[...] = b_ref[...]
    d_out[...] = d_ref[...]


def shards(tokens_in, grad_out, pre_act, w_in, w_out):
    vmem = pl.BlockSpec(memory_space=pltpu.VMEM)
    hbm = pl.BlockSpec(memory_space=pltpu.HBM)
    dma = pltpu.SemaphoreType.DMA
    shapes = (
        jax.ShapeDtypeStruct((ROWS, WIDE), bf16),
        jax.ShapeDtypeStruct((HID, DP), bf16),
        jax.ShapeDtypeStruct((HID, DP), bf16),
    )
    outs = pl.pallas_call(
        kernel,
        out_shape=shapes,
        in_specs=[hbm] * 5,
        out_specs=(vmem, vmem, vmem),
        scratch_shapes=[
            pltpu.VMEM((2, ROWS, WIDE), bf16),
            pltpu.VMEM((NX, ROWS, DQ), bf16),
            pltpu.VMEM((NX, ROWS, DQ), bf16),
            pltpu.VMEM((BLK, DQ), f32),
            pltpu.VMEM((2, NBLK, BLK, DQ), bf16),
            pltpu.VMEM((QR, QR), bf16),
            pltpu.VMEM((QR, HID), bf16),
            pltpu.VMEM((HID, WIDE), bf16),
            pltpu.VMEM((HID, WIDE), bf16),
            pltpu.VMEM((QR, HID), f32),
            pltpu.VMEM((NX, QR, HID), bf16),
            pltpu.VMEM((NX, QR, HID), bf16),
            pltpu.VMEM((QR, WIDE), bf16),
            pltpu.VMEM((NX * QR, DQ), bf16),
            pltpu.VMEM((NL, QR, DQ), bf16),
            pltpu.VMEM((2, NL, HID // 2, 2 * DP), bf16),
            pltpu.VMEM((2, HID // 2, 2 * DP), bf16),
            pltpu.VMEM((HID // 2, 2 * DP), bf16),
            pltpu.VMEM((HID // 2, 2 * DP), bf16),
            pltpu.VMEM((NX, HID // 2, 2 * DP), bf16),
            pltpu.VMEM((NW, QR, DQ), bf16),
            pltpu.VMEM((NC, NB, BLK, DQ), bf16),
            pltpu.VMEM((NB, BLK, DQ), bf16),
            pltpu.VMEM((2, NY // 2, NZ, BLK, DQ), bf16),
            pltpu.VMEM((2, NY // 2, NZ, BLK, DQ), bf16),
            pltpu.VMEM((BLK, DQ), f32),
            pltpu.VMEM((NZ, BLK, DQ), bf16),
            pltpu.VMEM((NZ, BLK, DQ), bf16),
            dma((200,)),
            dma((3,)),
            dma((2,)),
            dma((NX,)),
            dma((2, NZ)),
            dma((2, 2, NY // 2, NZ)),
            dma((2, NY)),
            dma((NX,)),
            dma((NX,)),
            dma((NL, 4)),
            dma((1,)),
            dma((NX, 4)),
            dma((2,)),
            dma((1,)),
            dma((NX,)),
            dma((2,)),
            dma((2, NY // 2, NZ)),
            dma((NZ,)),
        ],
        compiler_params=pltpu.CompilerParams(
            collective_id=0, has_side_effects=True, vmem_limit_bytes=60 * 1024 * 1024
        ),
        cost_estimate=pl.CostEstimate(
            flops=8 * 192 * 288 * 5120, bytes_accessed=4 * 1024 * 1024, transcendentals=0
        ),
        name="ffn_backward",
    )(grad_out, tokens_in, pre_act, w_out, w_in.T)
    grad_in, gwi, gwo = pl.pallas_call(
        deliver,
        out_shape=shapes,
        in_specs=[vmem] * 3,
        out_specs=(vmem,) * 3,
        compiler_params=pltpu.CompilerParams(vmem_limit_bytes=60 * 1024 * 1024),
        name="deliver",
    )(*outs)
    return grad_in, gwi.T, gwo


def solution(mesh):
    placed = (
        P(("tokens", "mp"), None),
        P(("tokens", "mp"), None),
        P("tokens", "mp"),
        P(None, "mp"),
        P("mp", None),
    )
    return jax.shard_map(
        shards,
        mesh=mesh,
        in_specs=placed,
        out_specs=(P(("tokens", "mp"), None), P("tokens", "mp"), P("mp", "tokens")),
        check_vma=False,
    )
```

```python
import math

import jax
import jax.numpy as jnp
from jax import lax
from jax.experimental import pallas as pl
from jax.experimental.pallas import tpu as pltpu
from jax.sharding import PartitionSpec as P

root_two_pi = math.sqrt(2.0 / math.pi)
cubic = 0.044715

NY, NZ, NC = 8, 3, 2
NL, NX = 4, 4
ROWS = 4
BLK = ROWS * NX
NB = NY * NZ
NBLK = NC * NB
QR = NBLK * ROWS
GRP = NBLK // 4
GR = GRP * ROWS
NW = 4
WIDE = 5120
HID = 288
DQ = WIDE // NX
DP = DQ // NL
NH = NZ * NL
HQ = DQ // NC
MESH = pl.DeviceIdType.MESH
f32 = jnp.float32
bf16 = jnp.bfloat16


def gelu_value(pre):
    inner = root_two_pi * (pre + cubic * pre * pre * pre)
    return 0.5 * pre * (1.0 + jnp.tanh(inner))


def gelu_slope(pre):
    tanh_val = jnp.tanh(root_two_pi * (pre + cubic * pre * pre * pre))
    return 0.5 * (1.0 + tanh_val) + 0.5 * pre * (1.0 - tanh_val * tanh_val) * root_two_pi * (
        1.0 + 3.0 * cubic * pre * pre
    )


def kernel(
    go_ref, ti_ref, pre_ref, wo_ref, wi_ref,
    gin_ref, gwi_ref, gwo_ref,
    rows_in, xsrc, xbuf, mbuf, gbuf, sel, prebuf, wo, wi, slope, act, gpbuf, cgo, cti, gw,
    wchunk, wpair, wfar, wlast, wx, gflat, gfold, grecv, rsend, rrecv, zown, zsend, zrecv,
    send_sem, in_sem, w_sem, x_sem, zg_sem, y_sem, sib_sem, act_sem, ag_sem, gw_sem, gwl_sem, gwsib_sem,
    wp_sem, wl_sem, wx_sem, gs_sem, ry_sem, rz_sem,
):
    m = lax.axis_index("mp")
    t = lax.axis_index("tokens")
    c = lax.rem(m, NC)
    zh = lax.rem(m // NC, NZ)
    y = m // (NC * NZ)
    x = lax.rem(t, NX)
    zl = t // NX
    sg = 1 - 2 * c

    def at(y_=None, zh_=None, c_=None, zl_=None, x_=None):
        y_ = y if y_ is None else y_
        zh_ = zh if zh_ is None else zh_
        c_ = c if c_ is None else c_
        zl_ = zl if zl_ is None else zl_
        x_ = x if x_ is None else x_
        return {"mp": (y_ * NZ + zh_) * NC + c_, "tokens": zl_ * NX + x_}

    def ring(v, n):
        return lax.rem(v + n, n)

    other = 1 - c
    xs = [lax.rem(x + d, NX) for d in range(1, NX)]
    zhs = [lax.rem(zh + d, NZ) for d in range(1, NZ)]
    zls = [lax.rem(zl + d, NL) for d in range(1, NL)]
    z = zh * NL + zl

    def along(d):
        z_ = lax.rem(z + d + NH, NH)
        return at(zh_=z_ // NL, zl_=lax.rem(z_, NL))

    near = zl + 1 - 2 * lax.rem(zl, 2)
    far_zl = lax.rem(zl + 2, NL)
    far_near = lax.rem(near + 2, NL)
    fwd = at(y_=ring(y + sg, NY))
    bwd = at(y_=ring(y - sg, NY))
    sib = at(c_=other)
    flying = []

    def send(src, dst, sem, dev):
        cp = pltpu.make_async_remote_copy(
            src_ref=src, dst_ref=dst, send_sem=send_sem.at[len(flying)], recv_sem=sem,
            device_id=dev, device_id_type=MESH,
        )
        cp.start()
        flying.append(cp)

    def arrive(dst, sem):
        pltpu.make_async_remote_copy(
            src_ref=dst, dst_ref=dst, send_sem=send_sem.at[0], recv_sem=sem,
            device_id=sib, device_id_type=MESH,
        ).wait_recv()

    first = [
        pltpu.make_async_copy(go_ref, rows_in.at[0], in_sem.at[0]),
        pltpu.make_async_copy(ti_ref, rows_in.at[1], in_sem.at[1]),
        pltpu.make_async_copy(pre_ref, prebuf, in_sem.at[2]),
    ]
    for cp in first:
        cp.start()

    barrier = pltpu.get_barrier_semaphore()
    peers = (
        [at(x_=v) for v in xs] + [along(d) for d in (1, 2, 3, 4, -1, -2, -3, -4)]
        + [fwd, bwd, sib]
    )
    for dev in peers:
        pl.semaphore_signal(barrier, inc=1, device_id=dev, device_id_type=MESH)

    loads = [
        pltpu.make_async_copy(wo_ref, wo, w_sem.at[0]),
        pltpu.make_async_copy(wi_ref, wi, w_sem.at[1]),
    ]
    for cp in loads:
        cp.start()

    def block(y_, zh_, c_):
        return c_ * NB + y_ * NZ + zh_

    first[0].wait()
    v = rows_in[0].astype(f32)
    for n in range(NW):
        mbuf[ROWS * n : ROWS * (n + 1)] = v[:, n * DQ : (n + 1) * DQ]
    gbuf[0, pl.ds(block(y, zh, c), 1)] = mbuf[...].astype(bf16)[None]
    first[1].wait()
    v = rows_in[1].astype(f32)
    for p in range(NX):
        xsrc[p] = jnp.concatenate(
            [v[:, k * DQ + p * DP : k * DQ + (p + 1) * DP] for k in range(NL)], axis=1
        ).astype(bf16)

    pl.semaphore_wait(barrier, len(peers))

    def spread(a):
        mine = gbuf.at[a, block(y, zh, c)]
        for v in zhs:
            send(mine, mine, zg_sem.at[a, zh], at(zh_=v))

    def hop(a, d, s, y_, zh_):
        ref = gbuf.at[a, block(y_, zh_, c)]
        send(ref, ref, y_sem.at[a, d, s, zh_], fwd if d == 0 else bwd)

    def to_sib(a, y_):
        ref = gbuf.at[a, pl.ds(block(y_, 0, c), NZ)]
        send(ref, ref, sib_sem.at[a, y_], sib)

    order = [zh] + zhs
    hops = (NY // 2, NY // 2 - 1)

    def ring_first(a, i):
        v = order[i]
        if i:
            ref = gbuf.at[a, block(y, v, c)]
            arrive(ref, zg_sem.at[a, v])
        hop(a, 0, 0, y, v)
        hop(a, 1, 0, y, v)
        if i == NZ - 1:
            to_sib(a, y)

    def ring_step(a, s):
        for i in range(NZ):
            v = order[i]
            for d in range(2):
                if s <= hops[d]:
                    y_ = ring(y - s * sg if d == 0 else y + s * sg, NY)
                    arrive(gbuf.at[a, block(y_, v, c)], y_sem.at[a, d, s - 1, v])
                    if s < hops[d]:
                        hop(a, d, s, y_, v)
                    if i == NZ - 1:
                        to_sib(a, y_)

    spread(0)
    ring_first(0, 0)
    for v in xs:
        send(xsrc.at[v], xbuf.at[x], x_sem.at[x], at(x_=v))
    xbuf[pl.ds(x, 1)] = xsrc[pl.ds(x, 1)]

    pairs = [(y, ring(y + 4, NY))] + [(ring(y + g, NY), ring(y - g, NY)) for g in range(1, 4)]
    i = lax.broadcasted_iota(jnp.int32, (QR, QR), 0)
    j = lax.broadcasted_iota(jnp.int32, (QR, QR), 1)

    n = (i >= GR).astype(jnp.int32) + (i >= 2 * GR).astype(jnp.int32) + (i >= 3 * GR).astype(jnp.int32)
    sel[...] = jnp.where(((i >> 2) - GRP * n) * BLK + n * ROWS + (i & 3) == j, 1.0, 0.0).astype(bf16)

    first[2].wait()
    q = (i * 43691) >> 19
    rest = i - 12 * q
    g = q >> 2
    ahead = jnp.where((q & 2) == 0, g, jnp.where(g == 0, 4, NY - g))
    src = ((y + ahead) & (NY - 1)) * (NZ * NC * ROWS) + (rest >> 2) * (NC * ROWS) + (q & 1) * ROWS + (rest & 3)
    hot = jnp.where(src == j, 1.0, 0.0).astype(bf16)
    pre = jnp.dot(hot, prebuf[...], preferred_element_type=f32)
    slope[...] = gelu_slope(pre)
    act[pl.ds(zl, 1)] = gelu_value(pre).astype(bf16)[None]

    ring_first(0, 1)
    ring_first(0, 2)

    for v in xs:
        arrive(xbuf.at[v], x_sem.at[v])
    for p in range(NX):
        mbuf[ROWS * p : ROWS * (p + 1)] = xbuf[p].astype(f32)
    gbuf[1, pl.ds(block(y, zh, c), 1)] = mbuf[...].astype(bf16)[None]
    spread(1)
    for v in zls:
        send(act.at[zl], act.at[zl], act_sem.at[zl], at(zl_=v))

    def group(a, g):
        for y_ in pairs[g]:
            arrive(gbuf.at[a, pl.ds(block(y_, 0, other), NZ)], sib_sem.at[a, y_])
        rows = [gbuf[a, pl.ds(block(y_, 0, c_), NZ)] for y_ in pairs[g] for c_ in range(NC)]
        return jnp.dot(
            sel[...], jnp.concatenate(rows, axis=0).reshape(QR, DQ), preferred_element_type=f32
        ).astype(bf16)

    def out_group(g):
        part = group(0, g)
        rows = slice(g * GR, (g + 1) * GR)
        for n in range(NW):
            cgo[rows, n * DQ : (n + 1) * DQ] = part[n * GR : (n + 1) * GR]

    def out_send(g):
        rows = slice(g * GR, (g + 1) * GR)
        for v, d in zip(zls, (1, 2 * sg, -1)):
            send(
                cgo.at[rows, cols(v * DQ + c * HQ)], gw.at[zl, rows, cols(c * HQ)], gw_sem.at[zl, g], along(d)
            )

    def cols(low):
        return pl.ds(pl.multiple_of(low, 128), HQ)

    def pass_on(g):
        rows = slice(g * GR, (g + 1) * GR)
        for v in zls:
            mine = gw.at[v, rows, cols(c * HQ)]
            arrive(mine, gw_sem.at[v, g])
            send(mine, mine, gwsib_sem.at[v, g], sib)

    ring_step(0, 1)
    ring_step(0, 2)
    out_group(1)
    out_send(1)
    ring_step(0, 3)
    out_group(2)
    out_send(2)
    ring_step(0, 4)
    for i in range(NZ):
        ring_first(1, i)
    out_group(3)
    out_group(0)

    for cp in loads:
        cp.wait()
    grad_act = lax.dot_general(
        cgo[...], wo[...], (((1,), (1,)), ((), ())), preferred_element_type=f32
    )
    gpbuf[pl.ds(x, 1)] = (grad_act * slope[...]).astype(bf16)[None]
    for v in xs:
        send(gpbuf.at[x], gpbuf.at[x], ag_sem.at[x], at(x_=v))

    ring_step(1, 1)

    grad_pre = gpbuf[pl.ds(x, 1)][0]
    for n in range(NW):
        part = jnp.dot(grad_pre, wi[:, n * DQ : (n + 1) * DQ], preferred_element_type=f32)
        gflat[n] = part.astype(bf16)
    for g in range(4):
        rows = gflat[:, g * GR : (g + 1) * GR, :].reshape(QR, DQ)
        part = lax.dot_general(
            sel[...], rows, (((0,), (0,)), ((), ())), preferred_element_type=f32
        ).astype(bf16).reshape(GRP, BLK, DQ)
        k = 0
        for y_ in pairs[g]:
            for c_ in range(NC):
                gfold[c_, pl.ds(y_ * NZ, NZ)] = part[k : k + NZ]
                k += NZ
    for h in range(2):
        some = pl.ds(h * (NB // 2), NB // 2)
        send(gfold.at[other, some], grecv.at[some], gs_sem.at[h], sib)

    ring_step(1, 2)
    out_send(3)
    out_send(0)
    own = pltpu.make_async_copy(
        cgo.at[:, pl.ds(pl.multiple_of(zl * DQ, 128), DQ)], gw.at[zl], gwl_sem.at[0]
    )
    own.start()

    for h in range(2):
        some = pl.ds(h * (NB // 2), NB // 2)
        arrive(grecv.at[some], gs_sem.at[h])

    def own_sum(y_, zh_):
        b = y_ * NZ + zh_
        return gfold[c, pl.ds(b, 1)][0].astype(f32) + grecv[pl.ds(b, 1)][0].astype(f32)

    def sum_step(s):
        for v in order:
            for d in range(2):
                if s <= hops[d]:
                    far = hops[d] + 1 - s
                    val = own_sum(ring(y + far * sg if d == 0 else y - far * sg, NY), v)
                    if s > 1:
                        arrive(rrecv.at[d, s - 2, v], ry_sem.at[d, s - 2, v])
                        val += rrecv[d, s - 2, pl.ds(v, 1)][0].astype(f32)
                    rsend[d, s - 1, pl.ds(v, 1)] = val.astype(bf16)[None]
                    send(
                        rsend.at[d, s - 1, v], rrecv.at[d, s - 1, v], ry_sem.at[d, s - 1, v],
                        fwd if d == 0 else bwd,
                    )

    scale_back = 1.0 / math.sqrt(NL * NX * NC * NB * ROWS)

    def weight_parts(a, lhs, right):
        for i in range(2):
            h = 1 - zl // 2 if i == 0 else zl // 2
            some = pl.ds(pl.multiple_of(2 * DP * h, 128), 2 * DP)
            rows = right[..., some].reshape(NX * QR, 2 * DP)
            part = scale_back * lax.dot_general(
                lhs, rows, (((0,), (0,)), ((), ())), preferred_element_type=f32
            )
            for k in range(2):
                put_chunk(a, 2 * h + k, part[:, k * DP : (k + 1) * DP])
            if a == 1 and i == 0:
                send(wchunk.at[a, far_near], wpair.at[1], wp_sem.at[1], at(zl_=near))

    def put_chunk(a, k, piece):
        whole = jnp.concatenate([piece[: HID // 2], piece[HID // 2 :]], axis=1).astype(bf16)
        wchunk[a, pl.ds(k, 1)] = whole[None]

    def weight_pair(a):
        dev = at(zl_=near)
        send(wchunk.at[a, near], wpair.at[0], wp_sem.at[0], dev)

    def weight_far(a):
        arrive(wpair.at[1], wp_sem.at[1])
        val = wchunk[a, pl.ds(far_zl, 1)][0].astype(f32) + wpair[1].astype(f32)
        wfar[...] = val.astype(bf16)
        send(wfar, wlast, wl_sem.at[0], at(zl_=far_zl))

    def put_sum(val, out):
        out[: HID // 2] = val[:, :DP].astype(bf16)
        out[HID // 2 :] = val[:, DP:].astype(bf16)

    def in_group(g):
        part = group(1, g)
        for p in range(NX):
            cti[p * QR + g * GR : p * QR + (g + 1) * GR] = part[p * GR : (p + 1) * GR]

    sum_step(1)
    ring_step(1, 3)
    in_group(1)
    sum_step(2)
    in_group(2)
    ring_step(1, 4)
    sum_step(3)
    in_group(3)
    in_group(0)

    for v in xs:
        arrive(gpbuf.at[v], ag_sem.at[v])
    weight_parts(1, gpbuf[...].reshape(NX * QR, HID), cti)
    weight_pair(1)
    pass_on(1)
    pass_on(2)
    sum_step(4)
    pass_on(3)
    pass_on(0)

    own.wait()
    for v in zls:
        arrive(act.at[v], act_sem.at[v])
        for g in range(4):
            arrive(gw.at[v, slice(g * GR, (g + 1) * GR), cols(other * HQ)], gwsib_sem.at[v, g])
    weight_parts(0, act[...].reshape(NX * QR, HID), gw)
    for v in xs:
        send(wchunk.at[0, v], wx.at[x], wx_sem.at[x], at(x_=v))

    weight_far(1)

    for i, v in enumerate(zhs + [zh]):
        val = own_sum(y, v)
        for d in range(2):
            s = hops[d] - 1
            arrive(rrecv.at[d, s, v], ry_sem.at[d, s, v])
            val += rrecv[d, s, pl.ds(v, 1)][0].astype(f32)
        if i == NZ - 1:
            zown[...] = val
        else:
            zsend[pl.ds(v, 1)] = val.astype(bf16)[None]
            send(zsend.at[v], zrecv.at[zh], rz_sem.at[zh], at(zh_=v))

    val = zown[...]
    for v in zhs:
        arrive(zrecv.at[v], rz_sem.at[v])
        val += zrecv[pl.ds(v, 1)][0].astype(f32)
    for n in range(NW):
        gin_ref[:, n * DQ : (n + 1) * DQ] = val[ROWS * n : ROWS * (n + 1)].astype(bf16)

    val = wchunk[0, pl.ds(x, 1)][0].astype(f32)
    for v in xs:
        arrive(wx.at[v], wx_sem.at[v])
        val += wx[pl.ds(v, 1)][0].astype(f32)
    put_sum(val, gwo_ref)

    arrive(wpair.at[0], wp_sem.at[0])
    val = wchunk[1, pl.ds(zl, 1)][0].astype(f32) + wpair[0].astype(f32)
    arrive(wlast, wl_sem.at[0])
    put_sum(val + wlast[...].astype(f32), gwi_ref)

    for cp in flying:
        cp.wait_send()


def deliver(a_ref, b_ref, d_ref, a_out, b_out, d_out):
    a_out[...] = a_ref[...]
    b_out[...] = b_ref[...]
    d_out[...] = d_ref[...]


def shards(tokens_in, grad_out, pre_act, w_in, w_out):
    vmem = pl.BlockSpec(memory_space=pltpu.VMEM)
    hbm = pl.BlockSpec(memory_space=pltpu.HBM)
    dma = pltpu.SemaphoreType.DMA
    shapes = (
        jax.ShapeDtypeStruct((ROWS, WIDE), bf16),
        jax.ShapeDtypeStruct((HID, DP), bf16),
        jax.ShapeDtypeStruct((HID, DP), bf16),
    )
    outs = pl.pallas_call(
        kernel,
        out_shape=shapes,
        in_specs=[hbm] * 5,
        out_specs=(vmem, vmem, vmem),
        scratch_shapes=[
            pltpu.VMEM((2, ROWS, WIDE), bf16),
            pltpu.VMEM((NX, ROWS, DQ), bf16),
            pltpu.VMEM((NX, ROWS, DQ), bf16),
            pltpu.VMEM((BLK, DQ), f32),
            pltpu.VMEM((2, NBLK, BLK, DQ), bf16),
            pltpu.VMEM((QR, QR), bf16),
            pltpu.VMEM((QR, HID), bf16),
            pltpu.VMEM((HID, WIDE), bf16),
            pltpu.VMEM((HID, WIDE), bf16),
            pltpu.VMEM((QR, HID), f32),
            pltpu.VMEM((NX, QR, HID), bf16),
            pltpu.VMEM((NX, QR, HID), bf16),
            pltpu.VMEM((QR, WIDE), bf16),
            pltpu.VMEM((NX * QR, DQ), bf16),
            pltpu.VMEM((NL, QR, DQ), bf16),
            pltpu.VMEM((2, NL, HID // 2, 2 * DP), bf16),
            pltpu.VMEM((2, HID // 2, 2 * DP), bf16),
            pltpu.VMEM((HID // 2, 2 * DP), bf16),
            pltpu.VMEM((HID // 2, 2 * DP), bf16),
            pltpu.VMEM((NX, HID // 2, 2 * DP), bf16),
            pltpu.VMEM((NW, QR, DQ), bf16),
            pltpu.VMEM((NC, NB, BLK, DQ), bf16),
            pltpu.VMEM((NB, BLK, DQ), bf16),
            pltpu.VMEM((2, NY // 2, NZ, BLK, DQ), bf16),
            pltpu.VMEM((2, NY // 2, NZ, BLK, DQ), bf16),
            pltpu.VMEM((BLK, DQ), f32),
            pltpu.VMEM((NZ, BLK, DQ), bf16),
            pltpu.VMEM((NZ, BLK, DQ), bf16),
            dma((200,)),
            dma((3,)),
            dma((2,)),
            dma((NX,)),
            dma((2, NZ)),
            dma((2, 2, NY // 2, NZ)),
            dma((2, NY)),
            dma((NX,)),
            dma((NX,)),
            dma((NL, 4)),
            dma((1,)),
            dma((NX, 4)),
            dma((2,)),
            dma((1,)),
            dma((NX,)),
            dma((2,)),
            dma((2, NY // 2, NZ)),
            dma((NZ,)),
        ],
        compiler_params=pltpu.CompilerParams(
            collective_id=0, has_side_effects=True, vmem_limit_bytes=60 * 1024 * 1024
        ),
        cost_estimate=pl.CostEstimate(
            flops=8 * 192 * 288 * 5120, bytes_accessed=4 * 1024 * 1024, transcendentals=0
        ),
        name="ffn_backward",
    )(grad_out, tokens_in, pre_act, w_out, w_in.T)
    grad_in, gwi, gwo = pl.pallas_call(
        deliver,
        out_shape=shapes,
        in_specs=[vmem] * 3,
        out_specs=(vmem,) * 3,
        compiler_params=pltpu.CompilerParams(vmem_limit_bytes=60 * 1024 * 1024),
        name="deliver",
    )(*outs)
    return grad_in, gwi.T, gwo


def solution(mesh):
    placed = (
        P(("tokens", "mp"), None),
        P(("tokens", "mp"), None),
        P("tokens", "mp"),
        P(None, "mp"),
        P("mp", None),
    )
    return jax.shard_map(
        shards,
        mesh=mesh,
        in_specs=placed,
        out_specs=(P(("tokens", "mp"), None), P("tokens", "mp"), P("mp", "tokens")),
        check_vma=False,
    )
```
